1024 devices in a mesh: pipe: 16 (over y, z_hi), tensor: 16 (over z_lo, core), dp: 4 (over x).
Axes of the slice: x: 4, y: 8, z: 16 (z_hi: 2, z_lo: 8; z = z_hi * 8 + z_lo), core: 2. Of those that a mesh axis runs over, the one named last changes fastest.
Arguments:
- out_grad: bfloat16 [16, 4, 128, 2560], P('pipe', 'dp', None, 'tensor'), may hold values from -6 to 6
- gate_pre: bfloat16 [16, 4, 13824, 128], P('pipe', 'dp', 'tensor'), may hold values from -6 to 6
- up_pre: bfloat16 [16, 4, 13824, 128], P('pipe', 'dp', 'tensor'), may hold values from -6 to 6
- down_weight: bfloat16 [16, 13824, 2560], P('pipe', 'tensor'), may hold values from -0.125 to 0.125
Outputs:
- gate_grad: bfloat16 [16, 4, 13824, 128], P('pipe', 'dp', 'tensor')
- up_grad: bfloat16 [16, 4, 13824, 128], P('pipe', 'dp', 'tensor')
- weight_grad: bfloat16 [16, 13824, 2560], P('pipe', 'tensor', 'dp')
The draws below stay inside these ranges and needn't reach their ends.
All inputs are finite; a program needn't handle non-finite values.
Results may differ from the reference program's by a relative error of at most 0.0075.
Values may be sent and summed in bfloat16 or wider, within the bound.
A program may use at most 64 MiB of HBM per device.

```python
import jax
import jax.numpy as jnp
from jax import lax

D_W = 2560
FF_W = 13824
TOK = 128
N_PIPE = 16
N_DP = 4


def block_scale(stream_key, dims, shards, low, top_value):
    gain, own = 1.0, jax.random.fold_in(stream_key, 6)
    for position, blocks in shards:
        draws = jnp.exp(jax.random.uniform(jax.random.fold_in(own, position), (blocks,), jnp.float32, low / len(shards), top_value / len(shards)))
        gain = gain * jnp.repeat(draws, dims[position] // blocks).reshape([-1 if axis == position else 1 for axis in range(len(dims))])
    return gain


def centred(stream_key, extent, scale, limit, cuts=(), kind=jnp.bfloat16):
    gain = block_scale(stream_key, extent, cuts, -0.22, 0.18) if cuts else 1.0
    array = jax.random.normal(stream_key, extent, jnp.float32) * scale * gain
    return jnp.minimum(jnp.maximum(array, -limit), limit).astype(kind)


def setup_inputs(seed: int = 0) -> dict:
    key_list = jax.random.split(jax.random.key(seed), 5)
    out_grad = centred(key_list[0], (N_PIPE, N_DP, TOK, D_W), 1.0, 6.0, ((0, 16), (1, 4), (3, 16)))
    gate_pre = centred(key_list[1], (N_PIPE, N_DP, FF_W, TOK), 1.0, 6.0, ((0, 16), (1, 4), (2, 16)))
    up_pre = centred(key_list[2], (N_PIPE, N_DP, FF_W, TOK), 1.0, 6.0, ((0, 16), (1, 4), (2, 16)))
    down_weight = centred(key_list[3], (N_PIPE, FF_W, D_W), D_W ** -0.5, 0.125, ((0, 16), (1, 16)))
    return {"out_grad": out_grad, "gate_pre": gate_pre, "up_pre": up_pre, "down_weight": down_weight}


def section_grads(inputs):
    grad_out, gate_in, up_in, weight = inputs
    gate_vals = gate_in.astype(jnp.float32)
    up_vals = up_in.astype(jnp.float32)
    sigmoid_gate = jax.nn.sigmoid(gate_vals)
    silu_gate = gate_vals * sigmoid_gate
    hidden = (silu_gate * up_vals).astype(jnp.bfloat16)
    hidden_grad = jnp.einsum("fd,rtd->rft", weight.astype(jnp.float32), grad_out.astype(jnp.float32))
    gate_grad = (hidden_grad * up_vals * sigmoid_gate * (1.0 + gate_vals * (1.0 - sigmoid_gate))).astype(jnp.bfloat16)
    up_grad = (hidden_grad * silu_gate).astype(jnp.bfloat16)
    replica_sum = jnp.einsum("rft,rtd->fd", hidden.astype(jnp.float32), grad_out.astype(jnp.float32))
    return gate_grad, up_grad, replica_sum.astype(jnp.bfloat16)


def reference(out_grad, gate_pre, up_pre, down_weight):
    gate_grad, up_grad, pair_term = lax.map(section_grads, (out_grad, gate_pre, up_pre, down_weight))
    partner_term = jnp.roll(pair_term, N_PIPE // 2, axis=0)
    grad_scale = 32.0 / (2.0 * N_DP * TOK)
    weight_grad = ((pair_term.astype(jnp.float32) + partner_term.astype(jnp.float32)) * grad_scale).astype(jnp.bfloat16)
    return (gate_grad, up_grad, weight_grad)
```

```python
import functools

import jax
import jax.numpy as jnp
from jax import lax
from jax.experimental import pallas as pl
from jax.experimental.pallas import tpu as pltpu
from jax.sharding import PartitionSpec as P

MESH = pl.DeviceIdType.MESH
CHUNKS = 3


def kernel(
    sizes,
    og_hbm, gate_hbm, up_hbm, weight_hbm,
    gg_hbm, ug_hbm, wg_hbm,
    og_in, gate, up, weight, og_all, wog, hid, acc, gg, ug, wg,
    local_sem, out_sem, og_send, og_recv, wog_send, wog_recv, hid_send, hid_recv,
):
    n_pipe, n_tensor, n_dp, rows, tok, width, scale = sizes
    p, t, x = lax.axis_index("pipe"), lax.axis_index("tensor"), lax.axis_index("dp")
    n_class = n_tensor // 4
    u, zr = lax.rem(t, 4), t // 4
    core = lax.rem(t, 2)
    sib = (p, t + 1 - 2 * core, x)
    near = (p, t + 2 - 4 * (u // 2), x)
    mirror = (lax.rem(p + n_pipe // 2, n_pipe), t, x)
    right = (p, t, lax.rem(x + 1, n_dp))
    left = (p, t, lax.rem(x + n_dp - 1, n_dp))
    across = (p, t, lax.rem(x + 2, n_dp))
    u_sib = u + 1 - 2 * core
    u_near = u + 2 - 4 * (u // 2)
    u_far = u_near + 1 - 2 * core
    mates = [lax.rem(zr + i, n_class) for i in range(n_class)]
    step = rows // CHUNKS
    half = step // 2

    loads = [
        pltpu.make_async_copy(og_hbm.at[0, 0], og_in, local_sem.at[0]),
        pltpu.make_async_copy(gate_hbm.at[0, 0], gate, local_sem.at[1]),
        pltpu.make_async_copy(up_hbm.at[0, 0], up, local_sem.at[2]),
        pltpu.make_async_copy(weight_hbm.at[0], weight, local_sem.at[3]),
    ]
    for load in loads:
        load.start()

    barrier = pltpu.get_barrier_semaphore()
    greeted = [sib, near, mirror, right, left, across] + [
        (p, 4 * r + u, x) for r in mates[1:]
    ]
    for device in greeted:
        pl.semaphore_signal(barrier, inc=1, device_id=device, device_id_type=MESH)

    def remote(src, dst, send, recv, device):
        return pltpu.make_async_remote_copy(
            src_ref=src, dst_ref=dst, send_sem=send, recv_sem=recv,
            device_id=device, device_id_type=MESH,
        )

    sent = []

    def send(src, dst, send_sem, recv_sem, device):
        copy = remote(src, dst, send_sem, recv_sem, device)
        copy.start()
        sent.append(copy)

    loads[0].wait()
    og_all[t] = og_in[...]

    loads[1].wait()
    loads[2].wait()

    def hidden_rows(i, carry):
        at = pl.ds(pl.multiple_of(i * half, half), half)
        g = gate[at, :].astype(jnp.float32)
        v = up[at, :].astype(jnp.float32)
        hid[0, 0, at, :] = (g * jax.nn.sigmoid(g) * v).astype(jnp.bfloat16)
        return carry

    lax.fori_loop(0, 2 * CHUNKS, hidden_rows, 0)

    pl.semaphore_wait(barrier, len(greeted))

    og_count = [0]

    def send_og(shard, device):
        n = og_count[0]
        og_count[0] += 1
        send(og_all.at[shard], og_all.at[shard], og_send.at[n], og_recv.at[shard], device)

    def wait_og(shard):
        remote(og_all.at[shard], og_all.at[shard], og_send.at[0], og_recv.at[shard], sib).wait_recv()

    wog_count = [0]

    def send_wog(q, k, v, src, q_to, device):
        n = wog_count[0]
        wog_count[0] += 1
        send(src, wog.at[q_to, k, v], wog_send.at[n], wog_recv.at[q_to, k, v], device)

    def wait_wog(q, k, v):
        remote(wog.at[q, k, v], wog.at[q, k, v], wog_send.at[0], wog_recv.at[q, k, v], sib).wait_recv()

    hid_count = [0]

    def send_hid(q, k, q_to, k_to, first, count, device):
        n = hid_count[0]
        hid_count[0] += 1
        at = pl.ds(first * half, count * half)
        send(
            hid.at[q, k, at], hid.at[q_to, k_to, at],
            hid_send.at[n], hid_recv.at[q_to, k_to, first], device,
        )

    def wait_hid(q, k, first, count):
        at = pl.ds(first * half, count * half)
        remote(
            hid.at[q, k, at], hid.at[q, k, at],
            hid_send.at[0], hid_recv.at[q, k, first], sib,
        ).wait_recv()

    def route_block(r):
        n = wog_count[0]
        wog_count[0] += 1
        shard = 4 * r + u
        k = lax.rem(x - r + n_dp, n_dp)

        @pl.when(r == x)
        def _():
            remote(og_all.at[shard], wog.at[1, 0, u], wog_send.at[n], wog_recv.at[1, 0, u], mirror).start()

        @pl.when(r != x)
        def _():
            remote(og_all.at[shard], wog.at[0, k, u], wog_send.at[n], wog_recv.at[0, k, u], (p, t, r)).start()

        sent.append(remote(og_all.at[shard], wog.at[0, 0, u], wog_send.at[n], wog_recv.at[0, 0, u], mirror))

    def take_mate(i):
        r = mates[i]
        if i:
            wait_og(4 * r + u)
        route_block(r)
        send_og(4 * r + u, near)
        send_og(4 * r + u, sib)

    def own_hidden(c):
        send_hid(0, 0, 0, n_dp - 1, 2 * c, 2, right)
        send_hid(0, 0, 0, 1, 2 * c, 2, left)
        send_hid(0, 0, 1, 0, 2 * c, 2, mirror)

    def relay_ring(q, c):
        wait_hid(q, 3, 2 * c, 2)
        send_hid(q, 3, q, 2, 2 * c, 1, right)
        wait_hid(q, 1, 2 * c, 2)
        send_hid(q, 1, q, 2, 2 * c + 1, 1, left)

    def relay_mirror(c):
        wait_hid(1, 0, 2 * c, 2)
        send_hid(1, 0, 1, n_dp - 1, 2 * c, 2, right)
        send_hid(1, 0, 1, 1, 2 * c, 2, left)

    for i in range(1, n_class):
        send_og(4 * zr + u, (p, 4 * mates[i] + u, x))
    take_mate(0)
    for c in range(CHUNKS):
        own_hidden(c)

    relay_ring(0, 0)
    take_mate(1)
    relay_ring(0, 1)
    take_mate(2)
    relay_ring(0, 2)
    relay_mirror(0)
    take_mate(3)
    for k in range(1, n_dp):
        wait_wog(0, k, u)
        send_wog(0, k, u, wog.at[0, k, u], 1, mirror)
        send_wog(0, k, u, wog.at[0, k, u], 0, near)
        send_wog(0, k, u, wog.at[0, k, u], 0, sib)
    relay_ring(1, 0)
    relay_mirror(1)
    for r in range(n_class):
        wait_og(4 * r + u_near)
        send_og(4 * r + u_near, sib)
    for k in range(1, n_dp):
        wait_wog(0, k, u_near)
        send_wog(0, k, u_near, wog.at[0, k, u_near], 0, sib)
    relay_ring(1, 1)
    relay_mirror(2)
    for r in range(n_class):
        wait_og(4 * r + u_sib)
        wait_og(4 * r + u_far)

    loads[3].wait()

    def projection_rows(i, carry):
        at = pl.ds(pl.multiple_of(i * half, half), half)
        grad = jnp.dot(
            weight[at, :], og_all[...].reshape(n_tensor * width, tok),
            preferred_element_type=jnp.float32,
        )
        g = gate[at, :].astype(jnp.float32)
        v = up[at, :].astype(jnp.float32)
        s = jax.nn.sigmoid(g)
        gg[at, :] = (grad * v * s * (1.0 + g * (1.0 - s))).astype(jnp.bfloat16)
        ug[at, :] = (grad * g * s).astype(jnp.bfloat16)
        return carry

    lax.fori_loop(0, 2 * CHUNKS, projection_rows, 0)
    outs = [
        pltpu.make_async_copy(gg, gg_hbm.at[0, 0], out_sem.at[0]),
        pltpu.make_async_copy(ug, ug_hbm.at[0, 0], out_sem.at[1]),
    ]
    for out in outs:
        out.start()

    for k in range(n_dp):
        wait_wog(1, k, u)
        send_wog(1, k, u, wog.at[1, k, u], 1, near)
        send_wog(1, k, u, wog.at[1, k, u], 1, sib)
    relay_ring(1, 2)

    for k in range(1, n_dp):
        wait_wog(0, k, u_sib)
        wait_wog(0, k, u_far)
    for first in range(2 * CHUNKS):
        wait_hid(0, 2, first, 1)

    def block_of(q, k):
        if q == 0 and k == 0:
            return og_all[pl.ds(4 * x, 4)].reshape(4 * width, tok)
        return wog[q, k].reshape(4 * width, tok)

    def term(q, at):
        left_side = jnp.concatenate([hid[q, k, at, :] for k in range(n_dp)], axis=1)
        right_side = jnp.concatenate([block_of(q, k) for k in range(n_dp)], axis=1)
        return lax.dot_general(
            left_side, right_side, (((1,), (1,)), ((), ())), preferred_element_type=jnp.float32
        )

    def own_rows(i, carry):
        at = pl.ds(pl.multiple_of(i * half, half), half)
        acc[at, :] = term(0, at)
        return carry

    lax.fori_loop(0, 2 * CHUNKS, own_rows, 0)

    for k in range(n_dp):
        wait_wog(1, k, u_near)
        send_wog(1, k, u_near, wog.at[1, k, u_near], 1, sib)
    for k in range(n_dp):
        wait_wog(1, k, u_sib)
        wait_wog(1, k, u_far)

    for c in range(CHUNKS):
        wait_hid(1, 2, 2 * c, 1)
        wait_hid(1, 2, 2 * c + 1, 1)

        def mirror_rows(i, carry):
            at = pl.ds(pl.multiple_of(i * half, half), half)
            wg[at, :] = ((acc[at, :] + term(1, at)) * scale).astype(jnp.bfloat16)
            return carry

        lax.fori_loop(2 * c, 2 * c + 2, mirror_rows, 0)
        at = pl.ds(c * step, step)
        out = pltpu.make_async_copy(wg.at[at], wg_hbm.at[0, at], out_sem.at[2 + c])
        out.start()
        outs.append(out)

    for copy in sent:
        copy.wait_send()
    for out in outs:
        out.wait()


def solution(mesh):
    n_pipe, n_tensor, n_dp = mesh.shape["pipe"], mesh.shape["tensor"], mesh.shape["dp"]

    def on_device(out_grad, gate_pre, up_pre, down_weight):
        tok, width = out_grad.shape[2:]
        rows = gate_pre.shape[2]
        full = down_weight.shape[2]
        cols = full // n_dp
        scale = 32.0 / (2.0 * n_dp * tok)
        sizes = (n_pipe, n_tensor, n_dp, rows, tok, width, scale)
        bf16, f32 = jnp.bfloat16, jnp.float32
        any_space = pl.BlockSpec(memory_space=pl.ANY)
        dma = pltpu.SemaphoreType.DMA
        return pl.pallas_call(
            functools.partial(kernel, sizes),
            out_shape=(
                jax.ShapeDtypeStruct((1, 1, rows, tok), bf16),
                jax.ShapeDtypeStruct((1, 1, rows, tok), bf16),
                jax.ShapeDtypeStruct((1, rows, cols), bf16),
            ),
            in_specs=[any_space] * 4,
            out_specs=(any_space,) * 3,
            scratch_shapes=[
                pltpu.VMEM((width, tok), bf16),
                pltpu.VMEM((rows, tok), bf16),
                pltpu.VMEM((rows, tok), bf16),
                pltpu.VMEM((rows, full), bf16),
                pltpu.VMEM((n_tensor, width, tok), bf16),
                pltpu.VMEM((2, n_dp, 4, width, tok), bf16),
                pltpu.VMEM((2, n_dp, rows, tok), bf16),
                pltpu.VMEM((rows, cols), f32),
                pltpu.VMEM((rows, tok), bf16),
                pltpu.VMEM((rows, tok), bf16),
                pltpu.VMEM((rows, cols), bf16),
                dma((4,)),
                dma((2 + CHUNKS,)),
                dma((16,)),
                dma((n_tensor,)),
                dma((40,)),
                dma((2, n_dp, 4)),
                dma((36,)),
                dma((2, n_dp, 2 * CHUNKS)),
            ],
            compiler_params=pltpu.CompilerParams(
                collective_id=0, has_side_effects=True, vmem_limit_bytes=60 * 2**20
            ),
        )(jnp.swapaxes(out_grad, 2, 3), gate_pre, up_pre, down_weight)

    in_specs = (
        P("pipe", "dp", None, "tensor"),
        P("pipe", "dp", "tensor", None),
        P("pipe", "dp", "tensor", None),
        P("pipe", "tensor", None),
    )
    out_specs = (
        P("pipe", "dp", "tensor", None),
        P("pipe", "dp", "tensor", None),
        P("pipe", "tensor", "dp"),
    )
    return jax.shard_map(
        on_device, mesh=mesh, in_specs=in_specs, out_specs=out_specs, check_vma=False
    )
```

```python
import functools

import jax
import jax.numpy as jnp
from jax import lax
from jax.experimental import pallas as pl
from jax.experimental.pallas import tpu as pltpu
from jax.sharding import PartitionSpec as P

MESH = pl.DeviceIdType.MESH
CHUNKS = 3


def kernel(
    sizes,
    og_hbm, gate_hbm, up_hbm, weight_hbm,
    gg, ug, wg,
    og_in, gate, up, weight, og_all, wog, hid, acc,
    local_sem, og_send, og_recv, block_send, wog_send, wog_recv, hid_send, hid_recv, ready,
):
    n_pipe, n_tensor, n_dp, rows, tok, width, scale = sizes
    p, t, x = lax.axis_index("pipe"), lax.axis_index("tensor"), lax.axis_index("dp")
    n_class = n_tensor // 4
    u, zr = lax.rem(t, 4), t // 4
    core = lax.rem(t, 2)
    sib = (p, t + 1 - 2 * core, x)
    near = (p, t + 2 - 4 * (u // 2), x)
    mirror = (lax.rem(p + n_pipe // 2, n_pipe), t, x)
    right = (p, t, lax.rem(x + 1, n_dp))
    left = (p, t, lax.rem(x + n_dp - 1, n_dp))
    ring = [(p, t, lax.rem(x + i, n_dp)) for i in range(1, n_dp)]
    mirror_ring = [(mirror[0], t, lax.rem(x + i, n_dp)) for i in range(1, n_dp)]
    u_sib = u + 1 - 2 * core
    u_near = u + 2 - 4 * (u // 2)
    u_far = u_near + 1 - 2 * core
    step = rows // CHUNKS
    half = step // 2

    loads = [
        pltpu.make_async_copy(og_hbm.at[0, 0], og_in, local_sem.at[0]),
        pltpu.make_async_copy(gate_hbm.at[0, 0], gate, local_sem.at[1]),
        pltpu.make_async_copy(up_hbm.at[0, 0], up, local_sem.at[2]),
        pltpu.make_async_copy(weight_hbm.at[0], weight, local_sem.at[3]),
    ]
    for load in loads:
        load.start()

    def signal(sem, device):
        pl.semaphore_signal(sem, inc=1, device_id=device, device_id_type=MESH)

    def mate(r):
        return (p, 4 * r + u, x)

    near_above = u < 2
    barrier = pltpu.get_barrier_semaphore()
    level = [sib, mirror] + ring + mirror_ring
    for device in level:
        signal(barrier, device)

    @pl.when(near_above)
    def _():
        signal(barrier, near)

    for r in range(n_class):
        @pl.when(r > zr)
        def _(r=r):
            signal(barrier, mate(r))

    def remote(src, dst, send, recv, device):
        return pltpu.make_async_remote_copy(
            src_ref=src, dst_ref=dst, send_sem=send, recv_sem=recv,
            device_id=device, device_id_type=MESH,
        )

    sent = []

    def send(src, dst, send_sem, recv_sem, device):
        copy = remote(src, dst, send_sem, recv_sem, device)
        copy.start()
        sent.append(copy)

    loads[0].wait()
    og_all[t] = og_in[...]

    loads[1].wait()
    loads[2].wait()

    def hidden_rows(i, carry):
        at = pl.ds(pl.multiple_of(i * half, half), half)
        g = gate[at, :].astype(jnp.float32)
        v = up[at, :].astype(jnp.float32)
        hid[0, 0, at, :] = (g * jax.nn.sigmoid(g) * v).astype(jnp.bfloat16)
        return carry

    lax.fori_loop(0, 2 * CHUNKS, hidden_rows, 0)

    pl.semaphore_wait(barrier, len(level) + u // 2 + zr)

    @pl.when(jnp.logical_not(near_above))
    def _():
        signal(ready.at[n_class], near)

    for r in range(n_class):
        @pl.when(r < zr)
        def _(r=r):
            signal(ready.at[zr], mate(r))

    def og_copy(shard, n, device):
        return remote(og_all.at[shard], og_all.at[shard], og_send.at[n], og_recv.at[shard], device)

    def wait_og(shard):
        og_copy(shard, 0, sib).wait_recv()

    wog_count = [0]

    def send_wog(q, k, v, src, q_to, device):
        n = wog_count[0]
        wog_count[0] += 1
        send(src, wog.at[q_to, k, v], wog_send.at[n], wog_recv.at[q_to, k, v], device)

    def wait_wog(q, k, v):
        remote(wog.at[q, k, v], wog.at[q, k, v], wog_send.at[0], wog_recv.at[q, k, v], sib).wait_recv()

    hid_count = [0]

    def send_hid(q, k, q_to, k_to, first, count, device):
        n = hid_count[0]
        hid_count[0] += 1
        at = pl.ds(first * half, count * half)
        send(
            hid.at[q, k, at], hid.at[q_to, k_to, at],
            hid_send.at[n], hid_recv.at[q_to, k_to, first], device,
        )

    def wait_hid(q, k, first, count):
        at = pl.ds(first * half, count * half)
        remote(
            hid.at[q, k, at], hid.at[q, k, at],
            hid_send.at[0], hid_recv.at[q, k, first], sib,
        ).wait_recv()

    def block_copies(r, n):
        shard = 4 * r + u
        k = lax.rem(x - r + n_dp, n_dp)
        return [
            remote(
                og_all.at[shard], wog.at[q, k, u], block_send.at[q, n], wog_recv.at[q, k, u],
                (lax.rem(p + q * (n_pipe // 2), n_pipe), t, r),
            )
            for q in range(2)
        ]

    def share(r, n):
        here, there = block_copies(r, n)

        @pl.when(r != x)
        def _():
            here.start()

        there.start()
        og_copy(4 * r + u, 3 * n, sib).start()

    def offer(d, when):
        r, n = zr + d, 3 + d

        @pl.when((r < n_class) & when)
        def _():
            pl.semaphore_wait(ready.at[r], 1)
            og_copy(4 * zr + u, 3 * n + 1, mate(r)).start()

    def take(d, when=True):
        r, n = zr + d, 3 + d

        @pl.when((r >= 0) & (r < n_class) & when)
        def _():
            wait_og(4 * r + u)
            share(r, n)
            og_copy(4 * r + u, 3 * n + 2, near).start()

    def took(d):
        r, n = zr + d, 3 + d

        @pl.when((r >= 0) & (r < n_class))
        def _():
            here, there = block_copies(r, n)

            @pl.when(r != x)
            def _():
                here.wait_send()

            there.wait_send()
            for i in range(2 if d == 0 else 3):
                og_copy(4 * r + u, 3 * n + (2 * i if d == 0 else i), sib).wait_send()

    def own_hidden(c):
        send_hid(0, 0, 1, 0, 2 * c, 2, mirror)
        send_hid(0, 0, 0, n_dp - 1, 2 * c, 2, right)
        send_hid(0, 0, 0, 1, 2 * c, 2, left)

    def relay_ring(q, c):
        wait_hid(q, 3, 2 * c, 2)
        send_hid(q, 3, q, 2, 2 * c, 1, right)
        wait_hid(q, 1, 2 * c, 2)
        send_hid(q, 1, q, 2, 2 * c + 1, 1, left)

    def relay_mirror(c):
        wait_hid(1, 0, 2 * c, 2)
        send_hid(1, 0, 1, n_dp - 1, 2 * c, 2, right)
        send_hid(1, 0, 1, 1, 2 * c, 2, left)

    for d in range(1 - n_class, 0):
        @pl.when(zr + d >= 0)
        def _(d=d):
            og_copy(4 * zr + u, 3 * (3 + d) + 1, mate(zr + d)).start()

    share(zr, 3)
    for c in range(CHUNKS):
        own_hidden(c)

    @pl.when(near_above)
    def _():
        pl.semaphore_wait(ready.at[n_class], 1)

    og_copy(4 * zr + u, 3 * 3 + 2, near).start()

    def relay_block(q, v):
        for k in range(1 - q, n_dp):
            wait_wog(q, k, v)
            if v is u:
                send_wog(q, k, v, wog.at[q, k, v], q, near)
            send_wog(q, k, v, wog.at[q, k, v], q, sib)

    together = lax.rem(p, 2) == 1
    apart = jnp.logical_not(together)

    for d in range(1, n_class):
        offer(d, together)
    relay_ring(0, 0)
    take(-1)
    offer(1, apart)
    take(1, together)
    relay_ring(0, 1)
    take(-2)
    take(2, together)
    take(1, apart)
    relay_mirror(0)
    relay_ring(0, 2)
    offer(2, apart)
    take(-3)
    take(3, together)
    relay_ring(1, 0)
    relay_mirror(1)
    take(2, apart)
    offer(3, apart)
    relay_ring(1, 1)
    relay_mirror(2)
    take(3, apart)
    relay_block(0, u)
    for r in range(n_class):
        wait_og(4 * r + u_near)
        n = 3 * (2 * n_class - 1) + r
        og_copy(4 * r + u_near, n, sib).start()
        sent.append(og_copy(4 * r + u_near, n, sib))
    relay_block(1, u)
    relay_block(0, u_near)

    for r in range(n_class):
        wait_og(4 * r + u_sib)
        wait_og(4 * r + u_far)
    loads[3].wait()

    def projection_rows(i, carry):
        at = pl.ds(pl.multiple_of(i * half, half), half)
        grad = jnp.dot(
            weight[at, :], og_all[...].reshape(n_tensor * width, tok),
            preferred_element_type=jnp.float32,
        )
        g = gate[at, :].astype(jnp.float32)
        v = up[at, :].astype(jnp.float32)
        s = jax.nn.sigmoid(g)
        gg[0, 0, at, :] = (grad * v * s * (1.0 + g * (1.0 - s))).astype(jnp.bfloat16)
        ug[0, 0, at, :] = (grad * g * s).astype(jnp.bfloat16)
        return carry

    lax.fori_loop(0, 2 * CHUNKS, projection_rows, 0)

    relay_ring(1, 2)
    relay_block(1, u_near)

    for k in range(1, n_dp):
        wait_wog(0, k, u_sib)
        wait_wog(0, k, u_far)
    for first in range(2 * CHUNKS):
        wait_hid(0, 2, first, 1)

    def block_of(q, k):
        if q == 0 and k == 0:
            return og_all[pl.ds(4 * x, 4)].reshape(4 * width, tok)
        return wog[q, k].reshape(4 * width, tok)

    def term(q, at):
        left_side = jnp.concatenate([hid[q, k, at, :] for k in range(n_dp)], axis=1)
        right_side = jnp.concatenate([block_of(q, k) for k in range(n_dp)], axis=1)
        return lax.dot_general(
            left_side, right_side, (((1,), (1,)), ((), ())), preferred_element_type=jnp.float32
        )

    def own_rows(i, carry):
        at = pl.ds(pl.multiple_of(i * half, half), half)
        acc[at, :] = term(0, at)
        return carry

    lax.fori_loop(0, 2 * CHUNKS, own_rows, 0)

    for k in range(n_dp):
        wait_wog(1, k, u_sib)
        wait_wog(1, k, u_far)

    for c in range(CHUNKS):
        wait_hid(1, 2, 2 * c, 1)
        wait_hid(1, 2, 2 * c + 1, 1)

        def mirror_rows(i, carry):
            at = pl.ds(pl.multiple_of(i * half, half), half)
            wg[0, at, :] = ((acc[at, :] + term(1, at)) * scale).astype(jnp.bfloat16)
            return carry

        lax.fori_loop(2 * c, 2 * c + 2, mirror_rows, 0)

    for copy in sent:
        copy.wait_send()
    for d in range(1 - n_class, n_class):
        took(d)


def write_out(gg, ug, wg, gg_out, ug_out, wg_out, sem):
    pairs = ((gg, gg_out), (ug, ug_out), (wg, wg_out))
    copies = [pltpu.make_async_copy(a, b, sem.at[i]) for i, (a, b) in enumerate(pairs)]
    for copy in copies:
        copy.start()
    for copy in copies:
        copy.wait()


def solution(mesh):
    n_pipe, n_tensor, n_dp = mesh.shape["pipe"], mesh.shape["tensor"], mesh.shape["dp"]

    def on_device(out_grad, gate_pre, up_pre, down_weight):
        tok, width = out_grad.shape[2:]
        rows = gate_pre.shape[2]
        full = down_weight.shape[2]
        cols = full // n_dp
        scale = 32.0 / (2.0 * n_dp * tok)
        sizes = (n_pipe, n_tensor, n_dp, rows, tok, width, scale)
        bf16, f32 = jnp.bfloat16, jnp.float32
        hbm = pl.BlockSpec(memory_space=pltpu.HBM)
        vmem = pl.BlockSpec(memory_space=pltpu.VMEM)
        dma = pltpu.SemaphoreType.DMA
        grads = pl.pallas_call(
            functools.partial(kernel, sizes),
            out_shape=(
                pltpu.VMEM((1, 1, rows, tok), bf16),
                pltpu.VMEM((1, 1, rows, tok), bf16),
                pltpu.VMEM((1, rows, cols), bf16),
            ),
            in_specs=[hbm] * 4,
            out_specs=(vmem,) * 3,
            scratch_shapes=[
                pltpu.VMEM((width, tok), bf16),
                pltpu.VMEM((rows, tok), bf16),
                pltpu.VMEM((rows, tok), bf16),
                pltpu.VMEM((rows, full), bf16),
                pltpu.VMEM((n_tensor, width, tok), bf16),
                pltpu.VMEM((2, n_dp, 4, width, tok), bf16),
                pltpu.VMEM((2, n_dp, rows, tok), bf16),
                pltpu.VMEM((rows, cols), f32),
                dma((4,)),
                dma((26,)),
                dma((n_tensor,)),
                dma((2, 7)),
                dma((24,)),
                dma((2, n_dp, 4)),
                dma((36,)),
                dma((2, n_dp, 2 * CHUNKS)),
                pltpu.SemaphoreType.REGULAR((5,)),
            ],
            compiler_params=pltpu.CompilerParams(
                collective_id=0, has_side_effects=True, vmem_limit_bytes=60 * 2**20
            ),
        )(jnp.swapaxes(out_grad, 2, 3), gate_pre, up_pre, down_weight)
        return pl.pallas_call(
            write_out,
            out_shape=[jax.ShapeDtypeStruct(g.shape, g.dtype) for g in grads],
            in_specs=[pl.BlockSpec(memory_space=pl.ANY)] * 3,
            out_specs=[hbm] * 3,
            scratch_shapes=[dma((3,))],
            compiler_params=pltpu.CompilerParams(vmem_limit_bytes=2**20),
        )(*grads)

    in_specs = (
        P("pipe", "dp", None, "tensor"),
        P("pipe", "dp", "tensor", None),
        P("pipe", "dp", "tensor", None),
        P("pipe", "tensor", None),
    )
    out_specs = (
        P("pipe", "dp", "tensor", None),
        P("pipe", "dp", "tensor", None),
        P("pipe", "tensor", "dp"),
    )
    return jax.shard_map(
        on_device, mesh=mesh, in_specs=in_specs, out_specs=out_specs, check_vma=False
    )
```

```python
import functools

import jax
import jax.numpy as jnp
from jax import lax
from jax.experimental import pallas as pl
from jax.experimental.pallas import tpu as pltpu
from jax.sharding import PartitionSpec as P

MESH = pl.DeviceIdType.MESH
PIECES = (9, 9, 9, 9, 9, 9)
CHUNKS = len(PIECES) // 2


def kernel(
    sizes,
    og_hbm, gate_hbm, up_hbm, weight_hbm,
    gg, ug, wg,
    og_in, gate, up, weight, og_all, wog, hid, acc,
    local_sem, og_send, og_recv, block_send, wog_send, wog_recv, hid_send, hid_recv, ready,
):
    n_pipe, n_tensor, n_dp, rows, tok, width, scale = sizes
    p, t, x = lax.axis_index("pipe"), lax.axis_index("tensor"), lax.axis_index("dp")
    n_class = n_tensor // 4
    u, zr = lax.rem(t, 4), t // 4
    core = lax.rem(t, 2)
    sib = (p, t + 1 - 2 * core, x)
    near = (p, t + 2 - 4 * (u // 2), x)
    mirror = (lax.rem(p + n_pipe // 2, n_pipe), t, x)
    right = (p, t, lax.rem(x + 1, n_dp))
    left = (p, t, lax.rem(x + n_dp - 1, n_dp))
    ring = [(p, t, lax.rem(x + i, n_dp)) for i in range(1, n_dp)]
    mirror_ring = [(mirror[0], t, lax.rem(x + i, n_dp)) for i in range(1, n_dp)]
    u_sib = u + 1 - 2 * core
    u_near = u + 2 - 4 * (u // 2)
    u_far = u_near + 1 - 2 * core
    unit = rows // sum(PIECES)
    starts = [unit * sum(PIECES[:i]) for i in range(len(PIECES) + 1)]
    tile = rows // 6

    def span(first, count=1):
        return pl.ds(starts[first], starts[first + count] - starts[first])

    loads = [
        pltpu.make_async_copy(og_hbm.at[0, 0], og_in, local_sem.at[0]),
        pltpu.make_async_copy(gate_hbm.at[0, 0], gate, local_sem.at[1]),
        pltpu.make_async_copy(up_hbm.at[0, 0], up, local_sem.at[2]),
        pltpu.make_async_copy(weight_hbm.at[0], weight, local_sem.at[3]),
    ]
    for load in loads:
        load.start()

    def signal(sem, device):
        pl.semaphore_signal(sem, inc=1, device_id=device, device_id_type=MESH)

    def mate(r):
        return (p, 4 * r + u, x)

    near_above = u < 2
    barrier = pltpu.get_barrier_semaphore()
    level = [sib, mirror] + ring + mirror_ring
    for device in level:
        signal(barrier, device)

    @pl.when(near_above)
    def _():
        signal(barrier, near)

    for r in range(n_class):
        @pl.when(r > zr)
        def _(r=r):
            signal(barrier, mate(r))

    def remote(src, dst, send, recv, device):
        return pltpu.make_async_remote_copy(
            src_ref=src, dst_ref=dst, send_sem=send, recv_sem=recv,
            device_id=device, device_id_type=MESH,
        )

    sent = []

    def send(src, dst, send_sem, recv_sem, device):
        copy = remote(src, dst, send_sem, recv_sem, device)
        copy.start()
        sent.append(copy)

    loads[0].wait()
    og_all[t] = og_in[...]

    loads[1].wait()
    loads[2].wait()

    def hidden_rows(i, carry):
        at = pl.ds(pl.multiple_of(i * tile, tile), tile)
        g = gate[at, :].astype(jnp.float32)
        v = up[at, :].astype(jnp.float32)
        hid[0, 0, at, :] = (g * jax.nn.sigmoid(g) * v).astype(jnp.bfloat16)
        return carry

    lax.fori_loop(0, rows // tile, hidden_rows, 0)

    pl.semaphore_wait(barrier, len(level) + u // 2 + zr)

    @pl.when(jnp.logical_not(near_above))
    def _():
        signal(ready.at[n_class], near)

    for r in range(n_class):
        @pl.when(r < zr)
        def _(r=r):
            signal(ready.at[zr], mate(r))

    def og_copy(shard, n, device):
        return remote(og_all.at[shard], og_all.at[shard], og_send.at[n], og_recv.at[shard], device)

    def wait_og(shard):
        og_copy(shard, 0, sib).wait_recv()

    wog_count = [0]

    def send_wog(q, k, v, src, q_to, device):
        n = wog_count[0]
        wog_count[0] += 1
        send(src, wog.at[q_to, k, v], wog_send.at[n], wog_recv.at[q_to, k, v], device)

    def wait_wog(q, k, v):
        remote(wog.at[q, k, v], wog.at[q, k, v], wog_send.at[0], wog_recv.at[q, k, v], sib).wait_recv()

    hid_count = [0]

    def send_hid(q, k, q_to, k_to, first, count, device):
        n = hid_count[0]
        hid_count[0] += 1
        at = span(first, count)
        send(
            hid.at[q, k, at], hid.at[q_to, k_to, at],
            hid_send.at[n], hid_recv.at[q_to, k_to, first], device,
        )

    def wait_hid(q, k, first, count):
        at = span(first, count)
        remote(
            hid.at[q, k, at], hid.at[q, k, at],
            hid_send.at[0], hid_recv.at[q, k, first], sib,
        ).wait_recv()

    def block_copies(r, n):
        shard = 4 * r + u
        k = lax.rem(x - r + n_dp, n_dp)
        return [
            remote(
                og_all.at[shard], wog.at[q, k, u], block_send.at[q, n], wog_recv.at[q, k, u],
                (lax.rem(p + q * (n_pipe // 2), n_pipe), t, r),
            )
            for q in range(2)
        ]

    def share(r, n):
        here, there = block_copies(r, n)

        @pl.when(r != x)
        def _():
            here.start()

        there.start()
        og_copy(4 * r + u, 3 * n, sib).start()

    def offer(d, when):
        r, n = zr + d, 3 + d

        @pl.when((r < n_class) & when)
        def _():
            pl.semaphore_wait(ready.at[r], 1)
            og_copy(4 * zr + u, 3 * n + 1, mate(r)).start()

    def take(d, when=True):
        r, n = zr + d, 3 + d

        @pl.when((r >= 0) & (r < n_class) & when)
        def _():
            wait_og(4 * r + u)
            share(r, n)
            og_copy(4 * r + u, 3 * n + 2, near).start()

    def took(d):
        r, n = zr + d, 3 + d

        @pl.when((r >= 0) & (r < n_class))
        def _():
            here, there = block_copies(r, n)

            @pl.when(r != x)
            def _():
                here.wait_send()

            there.wait_send()
            for i in range(2 if d == 0 else 3):
                og_copy(4 * r + u, 3 * n + (2 * i if d == 0 else i), sib).wait_send()

    def own_hidden(c):
        send_hid(0, 0, 1, 0, 2 * c, 2, mirror)
        send_hid(0, 0, 0, n_dp - 1, 2 * c, 2, right)
        send_hid(0, 0, 0, 1, 2 * c, 2, left)

    def relay_ring(q, c):
        wait_hid(q, 3, 2 * c, 2)
        send_hid(q, 3, q, 2, 2 * c, 1, right)
        wait_hid(q, 1, 2 * c, 2)
        send_hid(q, 1, q, 2, 2 * c + 1, 1, left)

    def relay_mirror(c):
        wait_hid(1, 0, 2 * c, 2)
        send_hid(1, 0, 1, n_dp - 1, 2 * c, 2, right)
        send_hid(1, 0, 1, 1, 2 * c, 2, left)

    for d in range(1 - n_class, 0):
        @pl.when(zr + d >= 0)
        def _(d=d):
            og_copy(4 * zr + u, 3 * (3 + d) + 1, mate(zr + d)).start()

    share(zr, 3)
    for c in range(CHUNKS):
        own_hidden(c)

    @pl.when(near_above)
    def _():
        pl.semaphore_wait(ready.at[n_class], 1)

    og_copy(4 * zr + u, 3 * 3 + 2, near).start()

    def relay_block(q, v):
        for k in range(1 - q, n_dp):
            wait_wog(q, k, v)
            if v is u:
                send_wog(q, k, v, wog.at[q, k, v], q, near)
            send_wog(q, k, v, wog.at[q, k, v], q, sib)

    together = lax.rem(p, 2) == 1
    apart = jnp.logical_not(together)

    for d in range(1, n_class):
        offer(d, together)
    relay_ring(0, 0)
    take(-1)
    offer(1, apart)
    take(1, together)
    relay_ring(0, 1)
    take(-2)
    take(2, together)
    take(1, apart)
    relay_mirror(0)
    for c in range(2, CHUNKS):
        relay_ring(0, c)
    offer(2, apart)
    take(-3)
    take(3, together)
    relay_ring(1, 0)
    relay_mirror(1)
    take(2, apart)
    offer(3, apart)
    for c in range(2, CHUNKS):
        relay_ring(1, c - 1)
        relay_mirror(c)
    take(3, apart)
    relay_block(0, u)
    for r in range(n_class):
        wait_og(4 * r + u_near)
        n = 3 * (2 * n_class - 1) + r
        og_copy(4 * r + u_near, n, sib).start()
        sent.append(og_copy(4 * r + u_near, n, sib))
    relay_block(1, u)
    relay_block(0, u_near)

    for r in range(n_class):
        wait_og(4 * r + u_sib)
        wait_og(4 * r + u_far)
    loads[3].wait()

    def projection_rows(i, carry):
        at = pl.ds(pl.multiple_of(i * tile, tile), tile)
        grad = jnp.dot(
            weight[at, :], og_all[...].reshape(n_tensor * width, tok),
            preferred_element_type=jnp.float32,
        )
        g = gate[at, :].astype(jnp.float32)
        v = up[at, :].astype(jnp.float32)
        s = jax.nn.sigmoid(g)
        gg[0, 0, at, :] = (grad * v * s * (1.0 + g * (1.0 - s))).astype(jnp.bfloat16)
        ug[0, 0, at, :] = (grad * g * s).astype(jnp.bfloat16)
        return carry

    lax.fori_loop(0, rows // tile, projection_rows, 0)

    relay_ring(1, CHUNKS - 1)
    relay_block(1, u_near)

    for k in range(1, n_dp):
        wait_wog(0, k, u_sib)
        wait_wog(0, k, u_far)
    for first in range(2 * CHUNKS):
        wait_hid(0, 2, first, 1)

    def block_of(q, k):
        if q == 0 and k == 0:
            return og_all[pl.ds(4 * x, 4)].reshape(4 * width, tok)
        return wog[q, k].reshape(4 * width, tok)

    def term(q, at):
        left_side = jnp.concatenate([hid[q, k, at, :] for k in range(n_dp)], axis=1)
        right_side = jnp.concatenate([block_of(q, k) for k in range(n_dp)], axis=1)
        return lax.dot_general(
            left_side, right_side, (((1,), (1,)), ((), ())), preferred_element_type=jnp.float32
        )

    def own_rows(i, carry):
        at = pl.ds(pl.multiple_of(i * tile, tile), tile)
        acc[at, :] = term(0, at)
        return carry

    lax.fori_loop(0, rows // tile, own_rows, 0)

    for k in range(n_dp):
        wait_wog(1, k, u_sib)
        wait_wog(1, k, u_far)

    for c in range(CHUNKS):
        wait_hid(1, 2, 2 * c, 1)
        wait_hid(1, 2, 2 * c + 1, 1)

        for piece in (2 * c, 2 * c + 1):
            at = span(piece)
            wg[0, at, :] = ((acc[at, :] + term(1, at)) * scale).astype(jnp.bfloat16)

    for copy in sent:
        copy.wait_send()
    for d in range(1 - n_class, n_class):
        took(d)


def write_out(gg, ug, wg, gg_out, ug_out, wg_out, sem):
    pairs = ((gg, gg_out), (ug, ug_out), (wg, wg_out))
    copies = [pltpu.make_async_copy(a, b, sem.at[i]) for i, (a, b) in enumerate(pairs)]
    for copy in copies:
        copy.start()
    for copy in copies:
        copy.wait()


def solution(mesh):
    n_pipe, n_tensor, n_dp = mesh.shape["pipe"], mesh.shape["tensor"], mesh.shape["dp"]

    def on_device(out_grad, gate_pre, up_pre, down_weight):
        tok, width = out_grad.shape[2:]
        rows = gate_pre.shape[2]
        full = down_weight.shape[2]
        cols = full // n_dp
        scale = 32.0 / (2.0 * n_dp * tok)
        sizes = (n_pipe, n_tensor, n_dp, rows, tok, width, scale)
        bf16, f32 = jnp.bfloat16, jnp.float32
        hbm = pl.BlockSpec(memory_space=pltpu.HBM)
        vmem = pl.BlockSpec(memory_space=pltpu.VMEM)
        dma = pltpu.SemaphoreType.DMA
        grads = pl.pallas_call(
            functools.partial(kernel, sizes),
            out_shape=(
                pltpu.VMEM((1, 1, rows, tok), bf16),
                pltpu.VMEM((1, 1, rows, tok), bf16),
                pltpu.VMEM((1, rows, cols), bf16),
            ),
            in_specs=[hbm] * 4,
            out_specs=(vmem,) * 3,
            scratch_shapes=[
                pltpu.VMEM((width, tok), bf16),
                pltpu.VMEM((rows, tok), bf16),
                pltpu.VMEM((rows, tok), bf16),
                pltpu.VMEM((rows, full), bf16),
                pltpu.VMEM((n_tensor, width, tok), bf16),
                pltpu.VMEM((2, n_dp, 4, width, tok), bf16),
                pltpu.VMEM((2, n_dp, rows, tok), bf16),
                pltpu.VMEM((rows, cols), f32),
                dma((4,)),
                dma((26,)),
                dma((n_tensor,)),
                dma((2, 7)),
                dma((24,)),
                dma((2, n_dp, 4)),
                dma((12 * CHUNKS,)),
                dma((2, n_dp, 2 * CHUNKS)),
                pltpu.SemaphoreType.REGULAR((5,)),
            ],
            compiler_params=pltpu.CompilerParams(
                collective_id=0, has_side_effects=True, vmem_limit_bytes=60 * 2**20
            ),
        )(jnp.swapaxes(out_grad, 2, 3), gate_pre, up_pre, down_weight)
        return pl.pallas_call(
            write_out,
            out_shape=[jax.ShapeDtypeStruct(g.shape, g.dtype) for g in grads],
            in_specs=[pl.BlockSpec(memory_space=pl.ANY)] * 3,
            out_specs=[hbm] * 3,
            scratch_shapes=[dma((3,))],
            compiler_params=pltpu.CompilerParams(vmem_limit_bytes=2**20),
        )(*grads)

    in_specs = (
        P("pipe", "dp", None, "tensor"),
        P("pipe", "dp", "tensor", None),
        P("pipe", "dp", "tensor", None),
        P("pipe", "tensor", None),
    )
    out_specs = (
        P("pipe", "dp", "tensor", None),
        P("pipe", "dp", "tensor", None),
        P("pipe", "tensor", "dp"),
    )
    return jax.shard_map(
        on_device, mesh=mesh, in_specs=in_specs, out_specs=out_specs, check_vma=False
    )
```
